512 devices in a mesh: dp: 16 (over y, z_hi, core), ctx: 32 (over x, z_lo).
Axes of the slice: x: 4, y: 4, z: 16 (z_hi: 2, z_lo: 8; z = z_hi * 8 + z_lo), core: 2. Of those that a mesh axis runs over, the one named last changes fastest.
Arguments:
- query_act: bfloat16 [16, 4096, 4096], P('dp', 'ctx'), may hold values from -6 to 6
- gated_input: bfloat16 [16, 4096, 4096], P('dp', 'ctx'), may hold values from -6 to 6
- out_grad: bfloat16 [16, 4096, 4096], P('dp', 'ctx'), may hold values from -6 to 6
- filter_taps: float32 [4096, 4096], P('dp', 'ctx'), may hold values from -0.09375 to 0.09375
Outputs:
- input_grad: bfloat16 [16, 4096, 4096], P('dp', 'ctx')
- taps_grad: float32 [4096, 4096], P('dp', 'ctx')
The draws below stay inside these ranges and needn't reach their ends.
All inputs are finite; a program needn't handle non-finite values.
Results may differ from the reference program's by a relative error of at most 0.0049.
Values may be sent and summed in bfloat16 or wider, within the bound.
No kernel may reach another device: no remote copies, remote signals or barrier semaphores. Data moves between devices by JAX's collectives and lax.ppermute only.
A program may use at most 128 MiB of HBM per device.

```python
import math
import jax
import jax.numpy as jnp
from jax import lax

D = 4096
SEQ = 4096
BATCH = 16


def steps_of(rng, shape, pieces, low, largest):
    loudness = 1.0
    for axis_at, parts in pieces:
        heights = jax.random.uniform(jax.random.fold_in(jax.random.fold_in(rng, 6), axis_at), (parts,), jnp.float32, low / len(pieces), largest / len(pieces))
        loudness = loudness * jnp.repeat(jnp.exp(heights), shape[axis_at] // parts).reshape((-1,) + (1,) * (len(shape) - 1 - axis_at))
    return loudness


def scatter_about(rng, extent, deviation, bound, pieces=(), kind=jnp.bfloat16):
    loudness = steps_of(rng, extent, pieces, -0.22, 0.18) if pieces else 1.0
    entries = jax.random.normal(rng, extent, jnp.float32) * deviation * loudness
    return jnp.minimum(jnp.maximum(entries, -bound), bound).astype(kind)


def setup_inputs(seed: int = 0) -> dict:
    seeds = jax.random.split(jax.random.key(seed), 5)
    query_act = scatter_about(seeds[0], (BATCH, SEQ, D), 1.0, 6.0, ((0, 16), (1, 32)))
    gated_input = scatter_about(seeds[1], (BATCH, SEQ, D), 1.0, 6.0, ((0, 16), (1, 32)))
    out_grad = scatter_about(seeds[2], (BATCH, SEQ, D), 1.0, 6.0, ((0, 16), (1, 32)))
    filter_taps = scatter_about(seeds[3], (SEQ, D), SEQ ** -0.5, 0.09375, ((0, 16), (1, 32)), jnp.float32)
    return {"query_act": query_act, "gated_input": gated_input, "out_grad": out_grad, "filter_taps": filter_taps}


def reference(query_act, gated_input, out_grad, filter_taps):
    fft_size = 2 * SEQ
    taps_spectrum = jnp.conj(jnp.fft.rfft(filter_taps, n=fft_size, axis=0))

    def one_sequence(partial_value, inputs):
        query_row, gated_row, grad_row = inputs
        product = (grad_row.astype(jnp.float32) * query_row.astype(jnp.float32)).astype(jnp.bfloat16)
        product = lax.optimization_barrier(product).astype(jnp.float32)
        product_spec = jnp.fft.rfft(product, n=fft_size, axis=0)
        gated_spec = jnp.fft.rfft(gated_row.astype(jnp.float32), n=fft_size, axis=0)
        grad_rows = jnp.fft.irfft(product_spec * taps_spectrum, n=fft_size, axis=0)[:SEQ]
        cross = jnp.fft.irfft(product_spec * jnp.conj(gated_spec), n=fft_size, axis=0)[:SEQ]
        return (partial_value + cross.astype(jnp.float32), grad_rows.astype(jnp.bfloat16))
    taps_total, input_grad = lax.scan(one_sequence, jnp.zeros((SEQ, D), jnp.float32), (query_act, gated_input, out_grad))
    return (input_grad, taps_total / math.sqrt(SEQ * BATCH))
```

```python
import functools
import math

import jax
import jax.numpy as jnp
import ml_dtypes
import numpy as np
from jax import lax
from jax.experimental import pallas as pl
from jax.experimental.pallas import tpu as pltpu
from jax.sharding import PartitionSpec as P

bf16 = jnp.bfloat16
f32 = jnp.float32
fine = 128
coarse = 32
group = 8
groups = fine // group
vmem_limit = 56 * 1024 * 1024


def split_table(table):
    high = table.astype(ml_dtypes.bfloat16)
    low = (table - high.astype(np.float64)).astype(ml_dtypes.bfloat16)
    return np.stack([high, low], 0)


@functools.lru_cache(maxsize=None)
def make_tables():
    k0 = np.arange(coarse)[:, None, None]
    q = np.arange(coarse)[None, :, None]
    j = np.arange(fine)[None, None, :]
    angle = 2.0 * np.pi * (((2 * k0 + 1) * (fine * q + j)) % 16384) / 16384.0
    parts = np.stack([np.cos(angle), -np.sin(angle)], 1)
    parts = parts.reshape(coarse, 2, coarse, groups, group)
    full = np.zeros((groups, coarse, 2, group, coarse, group))
    for lane in range(group):
        full[:, :, :, lane, :, lane] = np.transpose(parts[..., lane], (3, 0, 1, 2))
    full = full.reshape(groups, coarse * 2 * group, coarse * group)
    back = np.transpose(full, (0, 2, 1)) * (2.0 / 8192.0)
    angle = 2.0 * np.pi * (np.outer(np.arange(fine), np.arange(fine)) % fine) / fine
    cosine, sine = np.cos(angle), np.sin(angle)
    inner = np.block([[cosine, sine], [-sine, cosine]])
    return split_table(full), split_table(back), split_table(inner), split_table(inner.T)


def dot(a, b):
    return jnp.dot(a, b, preferred_element_type=f32)


def split(value):
    high = value.astype(bf16)
    return high, (value - high.astype(f32)).astype(bf16)


def dot3(table_high, table_low, value):
    high, low = split(value)
    return dot(table_high, high) + (dot(table_low, high) + dot(table_high, low))


def coarse_forward(x_ref, wide_ref, table_ref, mid_ref):
    def widen(q, carry):
        wide_ref[q] = x_ref[q].astype(f32)
        return carry

    lax.fori_loop(0, coarse, widen, 0, unroll=4)

    def step(g, carry):
        rows = pl.ds(pl.multiple_of(g * group, group), group)
        value = wide_ref[:, rows, :].reshape(coarse * group, fine).astype(bf16)
        result = dot(table_ref[0, g], value) + dot(table_ref[1, g], value)
        mid_ref[:, rows, :] = result.reshape(2 * coarse, group, fine)
        return carry

    lax.fori_loop(0, groups, step, 0, unroll=2)


def coarse_backward(mid_ref, back_ref, out_ref):
    def step(g, carry):
        rows = pl.ds(pl.multiple_of(g * group, group), group)
        value = mid_ref[:, rows, :].reshape(2 * coarse * group, fine)
        result = dot3(back_ref[0, g], back_ref[1, g], value)
        out_ref[:, rows, :] = result.reshape(coarse, group, fine)
        return carry

    lax.fori_loop(0, groups, step, 0, unroll=2)


def fine_forward(mid_ref, inner_ref, k):
    value = mid_ref[pl.ds(2 * k, 2)].reshape(2 * fine, fine)
    return dot3(inner_ref[0], inner_ref[1], value)


def times_conj(a, b):
    a_re, a_im, b_re, b_im = a[:fine], a[fine:], b[:fine], b[fine:]
    return jnp.concatenate([a_re * b_re + a_im * b_im, a_im * b_re - a_re * b_im], 0)


def spectrum_kernel(x_ref, table_ref, inner_ref, spec_ref, wide_ref, mid_ref):
    coarse_forward(x_ref, wide_ref, table_ref, mid_ref)

    def step(k, carry):
        spec_ref[k] = fine_forward(mid_ref, inner_ref, k)
        return carry

    lax.fori_loop(0, coarse, step, 0, unroll=2)


def grad_kernel(x_ref, taps_ref, table_ref, back_ref, inner_ref, outer_ref, y_ref, spec_ref, wide_ref, mid_ref):
    coarse_forward(x_ref, wide_ref, table_ref, mid_ref)

    def step(k, carry):
        spec = fine_forward(mid_ref, inner_ref, k)
        spec_ref[k] = spec
        result = dot3(outer_ref[0], outer_ref[1], times_conj(spec, taps_ref[k]))
        mid_ref[pl.ds(2 * k, 2)] = result.reshape(2, fine, fine)
        return carry

    lax.fori_loop(0, coarse, step, 0, unroll=2)
    coarse_backward(mid_ref, back_ref, wide_ref)

    def narrow(q, carry):
        y_ref[q] = wide_ref[q].astype(bf16)
        return carry

    lax.fori_loop(0, coarse, narrow, 0, unroll=4)


def cross_kernel(x_ref, prod_ref, table_ref, back_ref, inner_ref, outer_ref, y_ref, wide_ref, mid_ref):
    coarse_forward(x_ref, wide_ref, table_ref, mid_ref)

    def step(k, carry):
        spec = fine_forward(mid_ref, inner_ref, k)
        result = dot3(outer_ref[0], outer_ref[1], times_conj(prod_ref[k], spec))
        mid_ref[pl.ds(2 * k, 2)] = result.reshape(2, fine, fine)
        return carry

    lax.fori_loop(0, coarse, step, 0, unroll=2)
    coarse_backward(mid_ref, back_ref, y_ref)


scratch = [pltpu.VMEM((coarse, fine, fine), f32), pltpu.VMEM((2 * coarse, fine, fine), f32)]
spec_shape = jax.ShapeDtypeStruct((coarse, 2 * fine, fine), f32)
params = pltpu.CompilerParams(vmem_limit_bytes=vmem_limit)


def call(kernel, out_shape, flops, *args):
    in_bytes = sum(a.size * a.dtype.itemsize for a in args)
    return pl.pallas_call(
        kernel,
        out_shape=out_shape,
        scratch_shapes=scratch,
        compiler_params=params,
        cost_estimate=pl.CostEstimate(flops=flops, bytes_accessed=in_bytes, transcendentals=0),
    )(*args)


def product_kernel(grad_ref, query_ref, out_ref):
    value = (grad_ref[0].astype(f32) * query_ref[0].astype(f32)).astype(bf16)
    for i in range(out_ref.shape[0]):
        out_ref[i] = value[:, i * fine : (i + 1) * fine]


def block_kernel(value_ref, out_ref):
    for i in range(out_ref.shape[0]):
        out_ref[i] = value_ref[0, :, i * fine : (i + 1) * fine]


def unblock_kernel(value_ref, out_ref):
    for i in range(value_ref.shape[0]):
        out_ref[0, :, i * fine : (i + 1) * fine] = value_ref[i]


blocks_a_step = 8


def to_blocks(kernel, *args):
    wide = pl.BlockSpec((1, fine, blocks_a_step * fine), lambda i: (0, 0, i))
    return pl.pallas_call(
        kernel,
        grid=(coarse // blocks_a_step,),
        in_specs=[wide] * len(args),
        out_specs=pl.BlockSpec((blocks_a_step, fine, fine), lambda i: (i, 0, 0)),
        out_shape=jax.ShapeDtypeStruct((coarse, fine, fine), bf16),
        compiler_params=params,
    )(*args)


def from_blocks(value):
    return pl.pallas_call(
        unblock_kernel,
        grid=(coarse // blocks_a_step,),
        in_specs=[pl.BlockSpec((blocks_a_step, fine, fine), lambda i: (i, 0, 0))],
        out_specs=pl.BlockSpec((1, fine, blocks_a_step * fine), lambda i: (0, 0, i)),
        out_shape=jax.ShapeDtypeStruct((1, fine, coarse * fine), bf16),
        compiler_params=params,
    )(value)


def to_owners(blocks):
    return lax.all_to_all(blocks, "ctx", 0, 0, tiled=True)


def swap(value, bit):
    return lax.ppermute(value, "dp", [(i, i ^ bit) for i in range(16)])


def turn(value, by):
    return lax.ppermute(value, "dp", [(i, (i + 4 * by) % 16) for i in range(16)])


def place():
    index = lax.axis_index("dp")
    return index // 4, index // 2 % 2, index % 2


def pair(mine, other, bit):
    return jnp.where(bit == 0, jnp.stack([mine, other]), jnp.stack([other, mine]))


def gather_taps(taps):
    y, z_hi, core = place()
    both = pair(taps, swap(taps, 2), z_hi)
    both = pair(both, swap(both, 1), core)
    both = jnp.transpose(both, (1, 0, 2, 3))
    whole = jnp.zeros((4,) + both.shape, both.dtype)
    whole = lax.dynamic_update_index_in_dim(whole, both, y, 0)
    for by in (1, 3, 2):
        whole = lax.dynamic_update_index_in_dim(whole, turn(both, by), (y - by) % 4, 0)
    return whole.reshape(coarse, fine, fine)


def sum_over_dp(cross):
    y, z_hi, core = place()
    parts = cross.reshape(4, 2, 2, 256, fine)
    away = lax.dynamic_index_in_dim(parts, 1 - core, 2, keepdims=False)
    kept = lax.dynamic_index_in_dim(parts, core, 2, keepdims=False) + swap(away, 1)
    total = lax.dynamic_index_in_dim(kept, y, 0, keepdims=False)
    for by in (1, 3, 2):
        away = lax.dynamic_index_in_dim(kept, (y + by) % 4, 0, keepdims=False)
        total = total + turn(away.astype(bf16), by).astype(f32)
    away = lax.dynamic_index_in_dim(total, 1 - z_hi, 0, keepdims=False)
    return lax.dynamic_index_in_dim(total, z_hi, 0, keepdims=False) + swap(away.astype(bf16), 2).astype(f32)


def body(query_act, gated_input, out_grad, filter_taps):
    table, back, inner, outer = (jnp.asarray(t) for t in make_tables())
    product = to_owners(to_blocks(product_kernel, out_grad, query_act))
    gated = to_owners(to_blocks(block_kernel, gated_input))
    taps = gather_taps(filter_taps.astype(bf16))
    one = 2 * 256 * 256 * 256 * 32
    taps_spec = call(spectrum_kernel, spec_shape, 3 * one, taps, table, inner)
    grad_rows, prod_spec = call(
        grad_kernel,
        (jax.ShapeDtypeStruct((coarse, fine, fine), bf16), spec_shape),
        6 * one,
        product, taps_spec, table, back, inner, outer,
    )
    input_grad = from_blocks(to_owners(grad_rows))
    cross = call(
        cross_kernel,
        jax.ShapeDtypeStruct((coarse, fine, fine), f32),
        6 * one,
        gated, prod_spec, table, back, inner, outer,
    )
    return input_grad, sum_over_dp(cross) * (1.0 / 256.0)


def solution(mesh):
    in_specs = (P("dp", "ctx", None), P("dp", "ctx", None), P("dp", "ctx", None), P("dp", "ctx"))
    out_specs = (P("dp", "ctx", None), P("dp", "ctx"))
    return jax.shard_map(body, mesh=mesh, in_specs=in_specs, out_specs=out_specs, check_vma=False)
```

```python
import functools
import math

import jax
import jax.numpy as jnp
import ml_dtypes
import numpy as np
from jax import lax
from jax.experimental import pallas as pl
from jax.experimental.pallas import tpu as pltpu
from jax.sharding import PartitionSpec as P

bf16 = jnp.bfloat16
f32 = jnp.float32
fine = 128
coarse = 32
group = 8
groups = fine // group
unrolled = 8
vmem_limit = 56 * 1024 * 1024


def split_table(table):
    high = table.astype(ml_dtypes.bfloat16)
    low = (table - high.astype(np.float64)).astype(ml_dtypes.bfloat16)
    return np.concatenate([high, low, high], 1)


@functools.lru_cache(maxsize=None)
def make_tables():
    k0, q, j = np.arange(coarse), np.arange(coarse), np.arange(fine)
    angle = 2.0 * np.pi * (np.outer(2 * k0 + 1, q) % 128) / 128.0
    parts = np.stack([np.cos(angle), -np.sin(angle)], 1).reshape(2 * coarse, coarse)
    forward = np.kron(parts, np.eye(group))
    backward = forward.T * (2.0 / 8192.0)
    angle = 2.0 * np.pi * np.outer(2 * k0 + 1, j) / 16384.0
    twiddle = np.stack([np.cos(angle), np.sin(angle)], 1).astype(np.float32)
    twiddle = np.ascontiguousarray(np.broadcast_to(twiddle[..., None], twiddle.shape + (fine,)))
    angle = 2.0 * np.pi * (np.outer(j, j) % fine) / fine
    cosine, sine = np.cos(angle), np.sin(angle)
    inner = np.block([[cosine, sine], [-sine, cosine]])
    return split_table(forward), split_table(backward), twiddle, split_table(inner), split_table(inner.T)


def dot(a, b):
    return jnp.dot(a, b, preferred_element_type=f32)


def split_dot(table_ref, value):
    high = value.astype(bf16)
    low = (value - high.astype(f32)).astype(bf16)
    return dot(table_ref[...], jnp.concatenate([high, high, low], 0))


def copy(source, target, sem):
    return pltpu.make_async_copy(source, target, sem)


def coarse_forward(x_ref, forward_ref, mid_ref):
    depth = coarse * group

    def step(g, carry):
        rows = pl.ds(pl.multiple_of(g * 2 * group, 2 * group), 2 * group)
        value = x_ref[:, rows, :].astype(f32)
        value = [value[:, i * group : (i + 1) * group, :].reshape(depth, fine) for i in (0, 1)]
        value = jnp.concatenate(value, 1).astype(bf16)
        result = dot(forward_ref[:, :depth], value) + dot(forward_ref[:, depth : 2 * depth], value)
        result = [result[:, i * fine : (i + 1) * fine].reshape(2 * coarse, group, fine) for i in (0, 1)]
        mid_ref[:, rows, :] = jnp.concatenate(result, 1)
        return carry

    lax.fori_loop(0, groups // 2, step, 0, unroll=unrolled)


def coarse_backward(mid_ref, backward_ref, out_ref, out, sems):
    def sent(g):
        rows = pl.ds(pl.multiple_of(g * 2 * group, 2 * group), 2 * group)
        return rows, copy(out_ref.at[:, rows, :], out.at[:, rows, :], sems.at[g])

    def step(g, carry):
        rows, leaving = sent(g)
        value = mid_ref[:, rows, :]
        value = [value[:, i * group : (i + 1) * group, :].reshape(2 * coarse * group, fine) for i in (0, 1)]
        result = split_dot(backward_ref, jnp.concatenate(value, 1))
        result = [result[:, i * fine : (i + 1) * fine].reshape(coarse, group, fine) for i in (0, 1)]
        out_ref[:, rows, :] = jnp.concatenate(result, 1).astype(out_ref.dtype)
        leaving.start()
        return carry

    lax.fori_loop(0, groups // 2, step, 0, unroll=unrolled)

    def finish(g, carry):
        sent(g)[1].wait()
        return carry

    lax.fori_loop(0, groups // 2, finish, 0)


def fine_forward(mid_ref, twiddle_ref, inner_ref, k):
    turned = []
    for i in (0, 1):
        re, im = mid_ref[4 * k + 2 * i], mid_ref[4 * k + 2 * i + 1]
        cosine, sine = twiddle_ref[2 * k + i, 0], twiddle_ref[2 * k + i, 1]
        turned.append(jnp.concatenate([re * cosine + im * sine, im * cosine - re * sine], 0))
    return split_dot(inner_ref, jnp.concatenate(turned, 1))


def fine_backward(mid_ref, twiddle_ref, outer_ref, k, spec):
    result = split_dot(outer_ref, spec)
    for i in (0, 1):
        columns = slice(i * fine, (i + 1) * fine)
        re, im = result[:fine, columns], result[fine:, columns]
        cosine, sine = twiddle_ref[2 * k + i, 0], twiddle_ref[2 * k + i, 1]
        mid_ref[4 * k + 2 * i] = re * cosine - im * sine
        mid_ref[4 * k + 2 * i + 1] = re * sine + im * cosine


def times_conj(a, b):
    a_re, a_im, b_re, b_im = a[:fine], a[fine:], b[:fine], b[fine:]
    return jnp.concatenate([a_re * b_re + a_im * b_im, a_im * b_re - a_re * b_im], 0)


def load(hbm, vmem, sems):
    copies = [copy(h, v, sems.at[i]) for i, (h, v) in enumerate(zip(hbm, vmem))]
    for c in copies:
        c.start()
    return copies


def spectrum_kernel(x, forward, inner, twiddle, spec, *scratch):
    vmem, (spec_ref, mid_ref, sems, out_sems) = scratch[:4], scratch[4:]
    x_ref, forward_ref, inner_ref, twiddle_ref = vmem
    copies = load((x, forward, inner, twiddle), vmem, sems)
    copies[0].wait()
    copies[1].wait()
    coarse_forward(x_ref, forward_ref, mid_ref)
    copies[2].wait()
    copies[3].wait()

    def step(k, carry):
        spec_ref[k] = fine_forward(mid_ref, twiddle_ref, inner_ref, k)
        copy(spec_ref.at[k], spec.at[k], out_sems.at[k]).start()
        return carry

    lax.fori_loop(0, coarse // 2, step, 0, unroll=unrolled)

    def finish(k, carry):
        copy(spec_ref.at[k], spec.at[k], out_sems.at[k]).wait()
        return carry

    lax.fori_loop(0, coarse // 2, finish, 0)


def grad_kernel(x, forward, inner, twiddle, taps, outer, backward, y, spec, *scratch):
    vmem, (y_ref, spec_ref, mid_ref, sems, out_sems) = scratch[:7], scratch[7:]
    x_ref, forward_ref, inner_ref, twiddle_ref, taps_ref, outer_ref, backward_ref = vmem
    copies = load((x, forward, inner, twiddle, taps, outer, backward), vmem, sems)
    copies[0].wait()
    copies[1].wait()
    coarse_forward(x_ref, forward_ref, mid_ref)
    for c in copies[2:6]:
        c.wait()

    def step(k, carry):
        value = fine_forward(mid_ref, twiddle_ref, inner_ref, k)
        spec_ref[k] = value
        copy(spec_ref.at[k], spec.at[k], out_sems.at[k]).start()
        fine_backward(mid_ref, twiddle_ref, outer_ref, k, times_conj(value, taps_ref[k]))
        return carry

    lax.fori_loop(0, coarse // 2, step, 0, unroll=unrolled)
    copies[6].wait()
    coarse_backward(mid_ref, backward_ref, y_ref, y, sems)

    def finish(k, carry):
        copy(spec_ref.at[k], spec.at[k], out_sems.at[k]).wait()
        return carry

    lax.fori_loop(0, coarse // 2, finish, 0)


def cross_kernel(x, forward, inner, twiddle, prod, outer, backward, y, *scratch):
    vmem, (y_ref, mid_ref, sems) = scratch[:7], scratch[7:]
    x_ref, forward_ref, inner_ref, twiddle_ref, prod_ref, outer_ref, backward_ref = vmem
    copies = load((x, forward, inner, twiddle, prod, outer, backward), vmem, sems)
    copies[0].wait()
    copies[1].wait()
    coarse_forward(x_ref, forward_ref, mid_ref)
    for c in copies[2:6]:
        c.wait()

    def step(k, carry):
        value = fine_forward(mid_ref, twiddle_ref, inner_ref, k)
        fine_backward(mid_ref, twiddle_ref, outer_ref, k, times_conj(prod_ref[k], value))
        return carry

    lax.fori_loop(0, coarse // 2, step, 0, unroll=unrolled)
    copies[6].wait()
    coarse_backward(mid_ref, backward_ref, y_ref, y, sems)


block_shape = (coarse, fine, fine)
spec_shape = jax.ShapeDtypeStruct((coarse // 2, 2 * fine, 2 * fine), f32)
params = pltpu.CompilerParams(vmem_limit_bytes=vmem_limit)
anywhere = pl.BlockSpec(memory_space=pl.ANY)


def call(kernel, out_shape, flops, *args):
    results = jax.tree.leaves(out_shape)
    scratch = [pltpu.VMEM(a.shape, a.dtype) for a in list(args) + results]
    scratch += [pltpu.VMEM((2 * coarse, fine, fine), f32), pltpu.SemaphoreType.DMA((8,))]
    if spec_shape in results:
        scratch.append(pltpu.SemaphoreType.DMA((coarse // 2,)))
    return pl.pallas_call(
        kernel,
        out_shape=out_shape,
        in_specs=[anywhere] * len(args),
        out_specs=jax.tree.map(lambda _: anywhere, out_shape),
        scratch_shapes=scratch,
        compiler_params=params,
        cost_estimate=pl.CostEstimate(flops=flops, bytes_accessed=2**23, transcendentals=0),
    )(*args)


def product_kernel(grad_ref, query_ref, out_ref):
    value = (grad_ref[0].astype(f32) * query_ref[0].astype(f32)).astype(bf16)
    for i in range(out_ref.shape[0]):
        out_ref[i] = value[:, i * fine : (i + 1) * fine]


def block_kernel(value_ref, out_ref):
    for i in range(out_ref.shape[0]):
        out_ref[i] = value_ref[0, :, i * fine : (i + 1) * fine]


def unblock_kernel(value_ref, out_ref):
    for i in range(value_ref.shape[0]):
        out_ref[0, :, i * fine : (i + 1) * fine] = value_ref[i]


blocks_a_step = 16


def to_blocks(kernel, *args):
    wide = pl.BlockSpec((1, fine, blocks_a_step * fine), lambda i: (0, 0, i))
    return pl.pallas_call(
        kernel,
        grid=(coarse // blocks_a_step,),
        in_specs=[wide] * len(args),
        out_specs=pl.BlockSpec((blocks_a_step, fine, fine), lambda i: (i, 0, 0)),
        out_shape=jax.ShapeDtypeStruct((coarse, fine, fine), bf16),
        compiler_params=params,
    )(*args)


def from_blocks(value):
    return pl.pallas_call(
        unblock_kernel,
        grid=(coarse // blocks_a_step,),
        in_specs=[pl.BlockSpec((blocks_a_step, fine, fine), lambda i: (i, 0, 0))],
        out_specs=pl.BlockSpec((1, fine, blocks_a_step * fine), lambda i: (0, 0, i)),
        out_shape=jax.ShapeDtypeStruct((1, fine, coarse * fine), bf16),
        compiler_params=params,
    )(value)


def to_owners(blocks):
    return lax.all_to_all(blocks, "ctx", 0, 0, tiled=True)


def swap(value, bit):
    return lax.ppermute(value, "dp", [(i, i ^ bit) for i in range(16)])


def turn(value, by):
    return lax.ppermute(value, "dp", [(i, (i + 4 * by) % 16) for i in range(16)])


def place():
    index = lax.axis_index("dp")
    return index // 4, index // 2 % 2, index % 2


def pair(mine, other, bit):
    return jnp.where(bit == 0, jnp.stack([mine, other]), jnp.stack([other, mine]))


def gather_taps(both):
    y, _, core = place()
    both = pair(both, swap(both, 1), core)
    both = jnp.transpose(both, (1, 0, 2, 3))
    whole = jnp.zeros((4,) + both.shape, both.dtype)
    whole = lax.dynamic_update_index_in_dim(whole, both, y, 0)
    for by in (1, 3, 2):
        whole = lax.dynamic_update_index_in_dim(whole, turn(both, by), (y - by) % 4, 0)
    return whole.reshape(coarse, fine, fine)


def sum_over_dp(cross):
    y, z_hi, core = place()
    parts = cross.reshape(4, 2, 2, 256, fine)
    away = lax.dynamic_index_in_dim(parts, 1 - core, 2, keepdims=False)
    kept = lax.dynamic_index_in_dim(parts, core, 2, keepdims=False) + swap(away, 1)
    total = lax.dynamic_index_in_dim(kept, y, 0, keepdims=False)
    for by in (1, 3, 2):
        away = lax.dynamic_index_in_dim(kept, (y + by) % 4, 0, keepdims=False)
        total = total + turn(away.astype(bf16), by).astype(f32)
    away = lax.dynamic_index_in_dim(total, 1 - z_hi, 0, keepdims=False)
    return lax.dynamic_index_in_dim(total, z_hi, 0, keepdims=False) + swap(away.astype(bf16), 2).astype(f32)


def body(query_act, gated_input, out_grad, filter_taps):
    forward, backward, twiddle, inner, outer = (jnp.asarray(t) for t in make_tables())
    taps = filter_taps.astype(bf16)
    other = swap(taps, 2)
    product = to_owners(to_blocks(product_kernel, out_grad, query_act))
    gated = to_blocks(block_kernel, gated_input)
    product, other, gated = lax.optimization_barrier((product, other, gated))
    taps = gather_taps(pair(taps, other, place()[1]))
    one = 2 * 256 * 256 * 256 * 32
    taps_spec = call(spectrum_kernel, spec_shape, 3 * one, taps, forward, inner, twiddle)
    gated = to_owners(gated)
    grad_rows, prod_spec = call(
        grad_kernel,
        (jax.ShapeDtypeStruct((coarse, fine, fine), bf16), spec_shape),
        6 * one,
        product, forward, inner, twiddle, taps_spec, outer, backward,
    )
    input_grad = from_blocks(to_owners(grad_rows))
    cross = call(
        cross_kernel,
        jax.ShapeDtypeStruct((coarse, fine, fine), f32),
        6 * one,
        gated, forward, inner, twiddle, prod_spec, outer, backward,
    )
    return input_grad, sum_over_dp(cross) * (1.0 / 256.0)


def solution(mesh):
    in_specs = (P("dp", "ctx", None), P("dp", "ctx", None), P("dp", "ctx", None), P("dp", "ctx"))
    out_specs = (P("dp", "ctx", None), P("dp", "ctx"))
    return jax.shard_map(body, mesh=mesh, in_specs=in_specs, out_specs=out_specs, check_vma=False)
```

```python
import functools
import math

import jax
import jax.numpy as jnp
import ml_dtypes
import numpy as np
from jax import lax
from jax.experimental import pallas as pl
from jax.experimental.pallas import tpu as pltpu
from jax.sharding import PartitionSpec as P

bf16 = jnp.bfloat16
f32 = jnp.float32
fine = 128
coarse = 32
group = 8
groups = fine // group
unrolled = 8
vmem_limit = 56 * 1024 * 1024


def split_table(table):
    high = table.astype(ml_dtypes.bfloat16)
    low = (table - high.astype(np.float64)).astype(ml_dtypes.bfloat16)
    return np.concatenate([high, low, high], 1)


@functools.lru_cache(maxsize=None)
def make_tables():
    k0, q, j = np.arange(coarse), np.arange(coarse), np.arange(fine)
    angle = 2.0 * np.pi * (np.outer(2 * k0 + 1, q) % 128) / 128.0
    parts = np.stack([np.cos(angle), -np.sin(angle)], 1).reshape(2 * coarse, coarse)
    forward = np.kron(parts, np.eye(group))
    backward = forward.T * (2.0 / 8192.0)
    angle = 2.0 * np.pi * np.outer(2 * k0 + 1, j) / 16384.0
    twiddle = np.stack([np.cos(angle), np.sin(angle)], 1).astype(np.float32)
    twiddle = np.ascontiguousarray(np.broadcast_to(twiddle[..., None], twiddle.shape + (fine,)))
    angle = 2.0 * np.pi * (np.outer(j, j) % fine) / fine
    cosine, sine = np.cos(angle), np.sin(angle)
    inner = np.block([[cosine, sine], [-sine, cosine]])
    return split_table(forward), split_table(backward), twiddle, split_table(inner), split_table(inner.T)


def dot(a, b):
    return jnp.dot(a, b, preferred_element_type=f32)


def split_dot(table_ref, value):
    high = value.astype(bf16)
    low = (value - high.astype(f32)).astype(bf16)
    return dot(table_ref[...], jnp.concatenate([high, high, low], 0))


def copy(source, target, sem):
    return pltpu.make_async_copy(source, target, sem)


def coarse_forward(x_ref, forward_ref, mid_ref):
    depth = coarse * group

    def step(g, carry):
        rows = pl.ds(pl.multiple_of(g * 2 * group, 2 * group), 2 * group)
        value = x_ref[:, rows, :].astype(f32)
        value = [value[:, i * group : (i + 1) * group, :].reshape(depth, fine) for i in (0, 1)]
        value = jnp.concatenate(value, 1).astype(bf16)
        result = dot(forward_ref[:, :depth], value) + dot(forward_ref[:, depth : 2 * depth], value)
        result = [result[:, i * fine : (i + 1) * fine].reshape(2 * coarse, group, fine) for i in (0, 1)]
        mid_ref[:, rows, :] = jnp.concatenate(result, 1)
        return carry

    lax.fori_loop(0, groups // 2, step, 0, unroll=unrolled)


def coarse_backward(mid_ref, backward_ref, out_ref, out, sems):
    def sent(g):
        rows = pl.ds(pl.multiple_of(g * 2 * group, 2 * group), 2 * group)
        return rows, copy(out_ref.at[:, rows, :], out.at[:, rows, :], sems.at[g])

    def step(g, carry):
        rows, leaving = sent(g)
        value = mid_ref[:, rows, :]
        value = [value[:, i * group : (i + 1) * group, :].reshape(2 * coarse * group, fine) for i in (0, 1)]
        result = split_dot(backward_ref, jnp.concatenate(value, 1))
        result = [result[:, i * fine : (i + 1) * fine].reshape(coarse, group, fine) for i in (0, 1)]
        out_ref[:, rows, :] = jnp.concatenate(result, 1).astype(out_ref.dtype)
        leaving.start()
        return carry

    lax.fori_loop(0, groups // 2, step, 0, unroll=unrolled)

    def finish(g, carry):
        sent(g)[1].wait()
        return carry

    lax.fori_loop(0, groups // 2, finish, 0)


def fine_forward(mid_ref, twiddle_ref, inner_ref, k):
    turned = []
    for i in (0, 1):
        re, im = mid_ref[4 * k + 2 * i], mid_ref[4 * k + 2 * i + 1]
        cosine, sine = twiddle_ref[2 * k + i, 0], twiddle_ref[2 * k + i, 1]
        turned.append(jnp.concatenate([re * cosine + im * sine, im * cosine - re * sine], 0))
    return split_dot(inner_ref, jnp.concatenate(turned, 1))


def fine_backward(mid_ref, twiddle_ref, outer_ref, k, spec):
    result = split_dot(outer_ref, spec)
    for i in (0, 1):
        columns = slice(i * fine, (i + 1) * fine)
        re, im = result[:fine, columns], result[fine:, columns]
        cosine, sine = twiddle_ref[2 * k + i, 0], twiddle_ref[2 * k + i, 1]
        mid_ref[4 * k + 2 * i] = re * cosine - im * sine
        mid_ref[4 * k + 2 * i + 1] = re * sine + im * cosine


def times_conj(a, b):
    a_re, a_im, b_re, b_im = a[:fine], a[fine:], b[:fine], b[fine:]
    return jnp.concatenate([a_re * b_re + a_im * b_im, a_im * b_re - a_re * b_im], 0)


def load(hbm, vmem, sems):
    copies = [copy(h, v, sems.at[i]) for i, (h, v) in enumerate(zip(hbm, vmem))]
    for c in copies:
        c.start()
    return copies


def spectrum_kernel(x, forward, inner, twiddle, spec, *scratch):
    vmem, (spec_ref, mid_ref, sems, out_sems) = scratch[:4], scratch[4:]
    x_ref, forward_ref, inner_ref, twiddle_ref = vmem
    copies = load((x, forward, inner, twiddle), vmem, sems)
    copies[0].wait()
    copies[1].wait()
    coarse_forward(x_ref, forward_ref, mid_ref)
    copies[2].wait()
    copies[3].wait()

    def step(k, carry):
        spec_ref[k] = fine_forward(mid_ref, twiddle_ref, inner_ref, k)
        copy(spec_ref.at[k], spec.at[k], out_sems.at[k]).start()
        return carry

    lax.fori_loop(0, coarse // 2, step, 0, unroll=unrolled)

    def finish(k, carry):
        copy(spec_ref.at[k], spec.at[k], out_sems.at[k]).wait()
        return carry

    lax.fori_loop(0, coarse // 2, finish, 0)


def grad_kernel(x, forward, inner, twiddle, taps, outer, backward, y, spec, *scratch):
    vmem, (y_ref, spec_ref, mid_ref, sems, out_sems) = scratch[:7], scratch[7:]
    x_ref, forward_ref, inner_ref, twiddle_ref, taps_ref, outer_ref, backward_ref = vmem
    copies = load((x, forward, inner, twiddle, taps, outer, backward), vmem, sems)
    copies[0].wait()
    copies[1].wait()
    coarse_forward(x_ref, forward_ref, mid_ref)
    for c in copies[2:6]:
        c.wait()

    def step(k, carry):
        value = fine_forward(mid_ref, twiddle_ref, inner_ref, k)
        spec_ref[k] = value
        copy(spec_ref.at[k], spec.at[k], out_sems.at[k]).start()
        fine_backward(mid_ref, twiddle_ref, outer_ref, k, times_conj(value, taps_ref[k]))
        return carry

    lax.fori_loop(0, coarse // 2, step, 0, unroll=unrolled)
    copies[6].wait()
    coarse_backward(mid_ref, backward_ref, y_ref, y, sems)

    def finish(k, carry):
        copy(spec_ref.at[k], spec.at[k], out_sems.at[k]).wait()
        return carry

    lax.fori_loop(0, coarse // 2, finish, 0)


def cross_kernel(x, forward, inner, twiddle, prod, outer, backward, y, *scratch):
    vmem, (y_ref, mid_ref, sems) = scratch[:7], scratch[7:]
    x_ref, forward_ref, inner_ref, twiddle_ref, prod_ref, outer_ref, backward_ref = vmem
    copies = load((x, forward, inner, twiddle, prod, outer, backward), vmem, sems)
    copies[0].wait()
    copies[1].wait()
    coarse_forward(x_ref, forward_ref, mid_ref)
    for c in copies[2:6]:
        c.wait()

    def step(k, carry):
        value = fine_forward(mid_ref, twiddle_ref, inner_ref, k)
        fine_backward(mid_ref, twiddle_ref, outer_ref, k, times_conj(prod_ref[k], value))
        return carry

    lax.fori_loop(0, coarse // 2, step, 0, unroll=unrolled)
    copies[6].wait()
    coarse_backward(mid_ref, backward_ref, y_ref, y, sems)


block_shape = (coarse, fine, fine)
spec_shape = jax.ShapeDtypeStruct((coarse // 2, 2 * fine, 2 * fine), f32)
params = pltpu.CompilerParams(vmem_limit_bytes=vmem_limit)
anywhere = pl.BlockSpec(memory_space=pl.ANY)


def call(kernel, out_shape, flops, *args):
    results = jax.tree.leaves(out_shape)
    scratch = [pltpu.VMEM(a.shape, a.dtype) for a in list(args) + results]
    scratch += [pltpu.VMEM((2 * coarse, fine, fine), f32), pltpu.SemaphoreType.DMA((8,))]
    if spec_shape in results:
        scratch.append(pltpu.SemaphoreType.DMA((coarse // 2,)))
    return pl.pallas_call(
        kernel,
        out_shape=out_shape,
        in_specs=[anywhere] * len(args),
        out_specs=jax.tree.map(lambda _: anywhere, out_shape),
        scratch_shapes=scratch,
        compiler_params=params,
        cost_estimate=pl.CostEstimate(flops=flops, bytes_accessed=2**23, transcendentals=0),
    )(*args)


def product_kernel(grad_ref, query_ref, out_ref):
    value = (grad_ref[0].astype(f32) * query_ref[0].astype(f32)).astype(bf16)
    for i in range(out_ref.shape[0]):
        out_ref[i] = value[:, i * fine : (i + 1) * fine]


def block_kernel(value_ref, out_ref):
    for i in range(out_ref.shape[0]):
        out_ref[i] = value_ref[0, :, i * fine : (i + 1) * fine]


blocks_a_step = 16


def to_blocks(kernel, *args):
    wide = pl.BlockSpec((1, fine, blocks_a_step * fine), lambda i: (0, 0, i))
    return pl.pallas_call(
        kernel,
        grid=(coarse // blocks_a_step,),
        in_specs=[wide] * len(args),
        out_specs=pl.BlockSpec((blocks_a_step, fine, fine), lambda i: (i, 0, 0)),
        out_shape=jax.ShapeDtypeStruct((coarse, fine, fine), bf16),
        compiler_params=params,
    )(*args)


def from_blocks(value):
    return jnp.transpose(value, (1, 0, 2)).reshape(1, fine, coarse * fine)


def to_owners(blocks):
    return lax.all_to_all(blocks, "ctx", 0, 0, tiled=True)


def swap(value, bit):
    return lax.ppermute(value, "dp", [(i, i ^ bit) for i in range(16)])


def turn(value, by):
    return lax.ppermute(value, "dp", [(i, (i + 4 * by) % 16) for i in range(16)])


def place():
    index = lax.axis_index("dp")
    return index // 4, index // 2 % 2, index % 2


def pair(mine, other, bit):
    return jnp.where(bit == 0, jnp.stack([mine, other]), jnp.stack([other, mine]))


def gather_taps(both):
    y, _, core = place()
    both = pair(both, swap(both, 1), core)
    both = jnp.transpose(both, (1, 0, 2, 3))
    whole = jnp.zeros((4,) + both.shape, both.dtype)
    whole = lax.dynamic_update_index_in_dim(whole, both, y, 0)
    for by in (1, 3, 2):
        whole = lax.dynamic_update_index_in_dim(whole, turn(both, by), (y - by) % 4, 0)
    return whole.reshape(coarse, fine, fine)


def sum_over_dp(cross):
    y, z_hi, core = place()
    parts = cross.reshape(4, 2, 2, 256, fine)
    away = lax.dynamic_index_in_dim(parts, 1 - core, 2, keepdims=False)
    kept = lax.dynamic_index_in_dim(parts, core, 2, keepdims=False) + swap(away.astype(bf16), 1).astype(f32)
    total = lax.dynamic_index_in_dim(kept, y, 0, keepdims=False)
    for by in (1, 3, 2):
        away = lax.dynamic_index_in_dim(kept, (y + by) % 4, 0, keepdims=False)
        total = total + turn(away.astype(bf16), by).astype(f32)
    away = lax.dynamic_index_in_dim(total, 1 - z_hi, 0, keepdims=False)
    return lax.dynamic_index_in_dim(total, z_hi, 0, keepdims=False) + swap(away.astype(bf16), 2).astype(f32)


def body(query_act, gated_input, out_grad, filter_taps):
    forward, backward, twiddle, inner, outer = (jnp.asarray(t) for t in make_tables())
    taps = filter_taps.astype(bf16)
    other = swap(taps, 2)
    product = to_owners(to_blocks(product_kernel, out_grad, query_act))
    gated = to_blocks(block_kernel, gated_input)
    product, other, gated = lax.optimization_barrier((product, other, gated))
    taps = gather_taps(pair(taps, other, place()[1]))
    one = 2 * 256 * 256 * 256 * 32
    taps_spec = call(spectrum_kernel, spec_shape, 3 * one, taps, forward, inner, twiddle)
    gated = to_owners(gated)
    grad_rows, prod_spec = call(
        grad_kernel,
        (jax.ShapeDtypeStruct((coarse, fine, fine), bf16), spec_shape),
        6 * one,
        product, forward, inner, twiddle, taps_spec, outer, backward,
    )
    input_grad = from_blocks(to_owners(grad_rows))
    cross = call(
        cross_kernel,
        jax.ShapeDtypeStruct((coarse, fine, fine), f32),
        6 * one,
        gated, forward, inner, twiddle, prod_spec, outer, backward,
    )
    return input_grad, sum_over_dp(cross) * (1.0 / 256.0)


def solution(mesh):
    in_specs = (P("dp", "ctx", None), P("dp", "ctx", None), P("dp", "ctx", None), P("dp", "ctx"))
    out_specs = (P("dp", "ctx", None), P("dp", "ctx"))
    return jax.shard_map(body, mesh=mesh, in_specs=in_specs, out_specs=out_specs, check_vma=False)
```

```python
import functools
import math

import jax
import jax.numpy as jnp
import ml_dtypes
import numpy as np
from jax import lax
from jax.experimental import pallas as pl
from jax.experimental.pallas import tpu as pltpu
from jax.sharding import PartitionSpec as P

bf16 = jnp.bfloat16
f32 = jnp.float32
fine = 128
coarse = 32
group = 8
groups = fine // group
unrolled = 8
vmem_limit = 56 * 1024 * 1024


def split_table(table):
    high = table.astype(ml_dtypes.bfloat16)
    low = (table - high.astype(np.float64)).astype(ml_dtypes.bfloat16)
    return np.concatenate([high, low, high], 1)


@functools.lru_cache(maxsize=None)
def make_tables():
    k0, q, j = np.arange(coarse), np.arange(coarse), np.arange(fine)
    angle = 2.0 * np.pi * (np.outer(2 * k0 + 1, q) % 128) / 128.0
    parts = np.stack([np.cos(angle), -np.sin(angle)], 1).reshape(2 * coarse, coarse)
    forward = np.kron(parts, np.eye(group))
    backward = forward.T * (2.0 / 8192.0)
    angle = 2.0 * np.pi * np.outer(2 * k0 + 1, j) / 16384.0
    twiddle = np.stack([np.cos(angle), np.sin(angle)], 1).astype(np.float32)
    twiddle = np.ascontiguousarray(np.broadcast_to(twiddle[..., None], twiddle.shape + (fine,)))
    angle = 2.0 * np.pi * (np.outer(j, j) % fine) / fine
    cosine, sine = np.cos(angle), np.sin(angle)
    inner = np.block([[cosine, sine], [-sine, cosine]])
    return split_table(forward), split_table(backward), twiddle, split_table(inner), split_table(inner.T)


def dot(a, b):
    return jnp.dot(a, b, preferred_element_type=f32)


def split_dot(table_ref, value):
    high = value.astype(bf16)
    low = (value - high.astype(f32)).astype(bf16)
    return dot(table_ref[...], jnp.concatenate([high, high, low], 0))


def copy(source, target, sem):
    return pltpu.make_async_copy(source, target, sem)


def coarse_forward(x_ref, forward_ref, mid_ref):
    depth = coarse * group

    def step(g, carry):
        rows = pl.ds(pl.multiple_of(g * 2 * group, 2 * group), 2 * group)
        value = x_ref[:, rows, :].astype(f32)
        value = [value[:, i * group : (i + 1) * group, :].reshape(depth, fine) for i in (0, 1)]
        value = jnp.concatenate(value, 1).astype(bf16)
        result = dot(forward_ref[:, :depth], value) + dot(forward_ref[:, depth : 2 * depth], value)
        result = [result[:, i * fine : (i + 1) * fine].reshape(2 * coarse, group, fine) for i in (0, 1)]
        mid_ref[:, rows, :] = jnp.concatenate(result, 1)
        return carry

    lax.fori_loop(0, groups // 2, step, 0, unroll=unrolled)


def coarse_backward(mid_ref, backward_ref, out_ref, out, sems):
    def sent(g):
        rows = pl.ds(pl.multiple_of(g * 2 * group, 2 * group), 2 * group)
        return rows, copy(out_ref.at[:, rows, :], out.at[:, rows, :], sems.at[g])

    def step(g, carry):
        rows, leaving = sent(g)
        value = mid_ref[:, rows, :]
        value = [value[:, i * group : (i + 1) * group, :].reshape(2 * coarse * group, fine) for i in (0, 1)]
        result = split_dot(backward_ref, jnp.concatenate(value, 1))
        result = [result[:, i * fine : (i + 1) * fine].reshape(coarse, group, fine) for i in (0, 1)]
        out_ref[:, rows, :] = jnp.concatenate(result, 1).astype(out_ref.dtype)
        leaving.start()
        return carry

    lax.fori_loop(0, groups // 2, step, 0, unroll=unrolled)

    def finish(g, carry):
        sent(g)[1].wait()
        return carry

    lax.fori_loop(0, groups // 2, finish, 0)


def fine_forward(mid_ref, twiddle_ref, inner_ref, k):
    turned = []
    for i in (0, 1):
        re, im = mid_ref[4 * k + 2 * i], mid_ref[4 * k + 2 * i + 1]
        cosine, sine = twiddle_ref[2 * k + i, 0], twiddle_ref[2 * k + i, 1]
        turned.append(jnp.concatenate([re * cosine + im * sine, im * cosine - re * sine], 0))
    return split_dot(inner_ref, jnp.concatenate(turned, 1))


def fine_backward(mid_ref, twiddle_ref, outer_ref, k, spec):
    result = split_dot(outer_ref, spec)
    for i in (0, 1):
        columns = slice(i * fine, (i + 1) * fine)
        re, im = result[:fine, columns], result[fine:, columns]
        cosine, sine = twiddle_ref[2 * k + i, 0], twiddle_ref[2 * k + i, 1]
        mid_ref[4 * k + 2 * i] = re * cosine - im * sine
        mid_ref[4 * k + 2 * i + 1] = re * sine + im * cosine


def times_conj(a, b):
    a_re, a_im, b_re, b_im = a[:fine], a[fine:], b[:fine], b[fine:]
    return jnp.concatenate([a_re * b_re + a_im * b_im, a_im * b_re - a_re * b_im], 0)


def load(hbm, vmem, sems):
    copies = [copy(h, v, sems.at[i]) for i, (h, v) in enumerate(zip(hbm, vmem))]
    for c in copies:
        c.start()
    return copies


def spectrum_kernel(x, forward, inner, twiddle, spec, *scratch):
    vmem, (spec_ref, mid_ref, sems, out_sems) = scratch[:4], scratch[4:]
    x_ref, forward_ref, inner_ref, twiddle_ref = vmem
    copies = load((x, forward, inner, twiddle), vmem, sems)
    copies[0].wait()
    copies[1].wait()
    coarse_forward(x_ref, forward_ref, mid_ref)
    copies[2].wait()
    copies[3].wait()

    def step(k, carry):
        spec_ref[k] = fine_forward(mid_ref, twiddle_ref, inner_ref, k)
        copy(spec_ref.at[k], spec.at[k], out_sems.at[k]).start()
        return carry

    lax.fori_loop(0, coarse // 2, step, 0, unroll=unrolled)

    def finish(k, carry):
        copy(spec_ref.at[k], spec.at[k], out_sems.at[k]).wait()
        return carry

    lax.fori_loop(0, coarse // 2, finish, 0)


def grad_kernel(x, forward, inner, twiddle, taps, outer, backward, y, spec, *scratch):
    vmem, (y_ref, spec_ref, mid_ref, sems, out_sems) = scratch[:7], scratch[7:]
    x_ref, forward_ref, inner_ref, twiddle_ref, taps_ref, outer_ref, backward_ref = vmem
    copies = load((x, forward, inner, twiddle, taps, outer, backward), vmem, sems)
    copies[0].wait()
    copies[1].wait()
    coarse_forward(x_ref, forward_ref, mid_ref)
    for c in copies[2:6]:
        c.wait()

    def step(k, carry):
        value = fine_forward(mid_ref, twiddle_ref, inner_ref, k)
        spec_ref[k] = value
        copy(spec_ref.at[k], spec.at[k], out_sems.at[k]).start()
        fine_backward(mid_ref, twiddle_ref, outer_ref, k, times_conj(value, taps_ref[k]))
        return carry

    lax.fori_loop(0, coarse // 2, step, 0, unroll=unrolled)
    copies[6].wait()
    coarse_backward(mid_ref, backward_ref, y_ref, y, sems)

    def finish(k, carry):
        copy(spec_ref.at[k], spec.at[k], out_sems.at[k]).wait()
        return carry

    lax.fori_loop(0, coarse // 2, finish, 0)


def cross_kernel(x, forward, inner, twiddle, prod, outer, backward, y, *scratch):
    vmem, (y_ref, mid_ref, sems) = scratch[:7], scratch[7:]
    x_ref, forward_ref, inner_ref, twiddle_ref, prod_ref, outer_ref, backward_ref = vmem
    copies = load((x, forward, inner, twiddle, prod, outer, backward), vmem, sems)
    copies[0].wait()
    copies[1].wait()
    coarse_forward(x_ref, forward_ref, mid_ref)
    for c in copies[2:6]:
        c.wait()

    def step(k, carry):
        value = fine_forward(mid_ref, twiddle_ref, inner_ref, k)
        fine_backward(mid_ref, twiddle_ref, outer_ref, k, times_conj(prod_ref[k], value))
        return carry

    lax.fori_loop(0, coarse // 2, step, 0, unroll=unrolled)
    copies[6].wait()
    coarse_backward(mid_ref, backward_ref, y_ref, y, sems)


block_shape = (coarse, fine, fine)
spec_shape = jax.ShapeDtypeStruct((coarse // 2, 2 * fine, 2 * fine), f32)
params = pltpu.CompilerParams(vmem_limit_bytes=vmem_limit)
anywhere = pl.BlockSpec(memory_space=pl.ANY)


def call(kernel, out_shape, flops, *args):
    results = jax.tree.leaves(out_shape)
    scratch = [pltpu.VMEM(a.shape, a.dtype) for a in list(args) + results]
    scratch += [pltpu.VMEM((2 * coarse, fine, fine), f32), pltpu.SemaphoreType.DMA((8,))]
    if spec_shape in results:
        scratch.append(pltpu.SemaphoreType.DMA((coarse // 2,)))
    return pl.pallas_call(
        kernel,
        out_shape=out_shape,
        in_specs=[anywhere] * len(args),
        out_specs=jax.tree.map(lambda _: anywhere, out_shape),
        scratch_shapes=scratch,
        compiler_params=params,
        cost_estimate=pl.CostEstimate(flops=flops, bytes_accessed=2**23, transcendentals=0),
    )(*args)


def product_kernel(grad_ref, query_ref, out_ref):
    value = (grad_ref[0].astype(f32) * query_ref[0].astype(f32)).astype(bf16)
    for i in range(out_ref.shape[0]):
        out_ref[i] = value[:, i * fine : (i + 1) * fine]


def block_kernel(value_ref, out_ref):
    for i in range(out_ref.shape[0]):
        out_ref[i] = value_ref[0, :, i * fine : (i + 1) * fine]


blocks_a_step = 16


def to_blocks(kernel, *args):
    wide = pl.BlockSpec((1, fine, blocks_a_step * fine), lambda i: (0, 0, i))
    return pl.pallas_call(
        kernel,
        grid=(coarse // blocks_a_step,),
        in_specs=[wide] * len(args),
        out_specs=pl.BlockSpec((blocks_a_step, fine, fine), lambda i: (i, 0, 0)),
        out_shape=jax.ShapeDtypeStruct((coarse, fine, fine), bf16),
        compiler_params=params,
    )(*args)


def from_blocks(value):
    return jnp.transpose(value, (1, 0, 2)).reshape(1, fine, coarse * fine)


def to_owners(blocks):
    return lax.all_to_all(blocks, "ctx", 0, 0, tiled=True)


def swap(value, bit):
    return lax.ppermute(value, "dp", [(i, i ^ bit) for i in range(16)])


def place():
    index = lax.axis_index("dp")
    return index // 4, index // 2 % 2, index % 2


def pair(mine, other, bit):
    return jnp.where(bit == 0, jnp.stack([mine, other]), jnp.stack([other, mine]))


def gather_taps(both):
    y, _, core = place()
    both = pair(both, swap(both, 1), core)
    both = jnp.transpose(both, (1, 0, 2, 3))
    whole = jnp.zeros((4,) + both.shape, both.dtype)
    whole = lax.dynamic_update_index_in_dim(whole, both, y, 0)
    for by in (1, 3, 2):
        whole = lax.dynamic_update_index_in_dim(whole, swap(both, 4 * by), y ^ by, 0)
    return whole.reshape(coarse, fine, fine)


def sum_over_dp(cross):
    y, z_hi, core = place()
    parts = cross.reshape(4, 2, 2, 256, fine)
    away = lax.dynamic_index_in_dim(parts, 1 - core, 2, keepdims=False)
    kept = lax.dynamic_index_in_dim(parts, core, 2, keepdims=False) + swap(away.astype(bf16), 1).astype(f32)
    total = lax.dynamic_index_in_dim(kept, y, 0, keepdims=False)
    for by in (1, 3, 2):
        away = lax.dynamic_index_in_dim(kept, y ^ by, 0, keepdims=False)
        total = total + swap(away.astype(bf16), 4 * by).astype(f32)
    away = lax.dynamic_index_in_dim(total, 1 - z_hi, 0, keepdims=False)
    return lax.dynamic_index_in_dim(total, z_hi, 0, keepdims=False) + swap(away.astype(bf16), 2).astype(f32)


def body(query_act, gated_input, out_grad, filter_taps):
    forward, backward, twiddle, inner, outer = (jnp.asarray(t) for t in make_tables())
    taps = filter_taps.astype(bf16)
    other = swap(taps, 2)
    product = to_owners(to_blocks(product_kernel, out_grad, query_act))
    gated = to_blocks(block_kernel, gated_input)
    product, other, gated = lax.optimization_barrier((product, other, gated))
    taps = gather_taps(pair(taps, other, place()[1]))
    one = 2 * 256 * 256 * 256 * 32
    taps_spec = call(spectrum_kernel, spec_shape, 3 * one, taps, forward, inner, twiddle)
    gated = to_owners(gated)
    grad_rows, prod_spec = call(
        grad_kernel,
        (jax.ShapeDtypeStruct((coarse, fine, fine), bf16), spec_shape),
        6 * one,
        product, forward, inner, twiddle, taps_spec, outer, backward,
    )
    input_grad = from_blocks(to_owners(grad_rows))
    cross = call(
        cross_kernel,
        jax.ShapeDtypeStruct((coarse, fine, fine), f32),
        6 * one,
        gated, forward, inner, twiddle, prod_spec, outer, backward,
    )
    return input_grad, sum_over_dp(cross) * (1.0 / 256.0)


def solution(mesh):
    in_specs = (P("dp", "ctx", None), P("dp", "ctx", None), P("dp", "ctx", None), P("dp", "ctx"))
    out_specs = (P("dp", "ctx", None), P("dp", "ctx"))
    return jax.shard_map(body, mesh=mesh, in_specs=in_specs, out_specs=out_specs, check_vma=False)
```
